32 devices in a mesh: dp: 16 (over z, y, core), mp: 2 (over x).
Axes of the slice: x: 2, y: 2, z: 4, core: 2. Of those that a mesh axis runs over, the one named last changes fastest.
Arguments:
- views: bfloat16 [8192, 256], P('dp'), may hold values from -1 to 1
- partner: int32 [8192], P('dp'), may hold values from 0 to 8191, as said below
- weight: float32 [8192], P('dp'), may hold values from 0.25 to 4
Outputs:
- loss: float32 [8192], P('dp')
- grad: float32 [8192, 256], P('dp')
The draws below stay inside these ranges and needn't reach their ends.
Inputs may be any that keep to these rules, and one draw needn't show every extreme that they name: partner pairs the views: partner[partner[i]] = i and partner[i] != i.
All inputs are finite; a program needn't handle non-finite values.
Results may differ from the reference program's by a relative error of at most 0.0056.
Values may be sent and summed in bfloat16 or wider, within the bound.
A program may use at most 64 MiB of HBM per device.

```python
import math
import jax
import jax.numpy as jnp
from jax import lax

W = 256
NV = 8192


def pairing(key):
    return jax.random.permutation(jax.random.fold_in(key, 7), NV).astype(jnp.int32)


def draw_partner(key, part):
    order = pairing(key)
    first = order[0::2]
    second = order[1::2]
    paired = jnp.zeros((NV,), jnp.int32)
    paired = paired.at[first].set(second)
    paired = paired.at[second].set(first)
    return paired


def noise_part(key, shape):
    return jax.random.truncated_normal(key, -4.0, 4.0, shape, jnp.float32)


def draw_views(key, part):
    order = pairing(key)
    image = jnp.zeros((NV,), jnp.int32).at[order].set(jnp.arange(NV, dtype=jnp.int32) // 2)
    groups = max(NV // 64, 4)
    images = NV // 2
    label = jax.random.randint(jax.random.fold_in(key, 11), (images,), 0, groups).astype(jnp.int32)
    tight = jax.random.uniform(jax.random.fold_in(key, 12), (groups,), jnp.float32, 0.1, 0.8)
    close = jax.random.uniform(jax.random.fold_in(key, 13), (images,), jnp.float32, 0.82, 0.95)
    view_label = label[image]
    class_share = tight[view_label]
    image_share = close[image] - class_share
    own_share = 1.0 - close[image]
    centres = noise_part(jax.random.fold_in(key, 21), (groups, W))
    image_dirs = noise_part(jax.random.fold_in(key, 22), (images, W))
    own = noise_part(jax.random.fold_in(key, 23), (NV, W))
    mixed = jnp.sqrt(class_share)[:, None] * centres[view_label]
    mixed = mixed + jnp.sqrt(image_share)[:, None] * image_dirs[image]
    mixed = mixed + jnp.sqrt(own_share)[:, None] * own
    common = noise_part(jax.random.fold_in(key, 24), (W,))
    loading = jax.random.uniform(jax.random.fold_in(key, 26), (NV,), jnp.float32, 0.0, 0.4)
    scale = jnp.exp(jax.random.uniform(jax.random.fold_in(key, 25), (NV,), jnp.float32, math.log(0.5), math.log(2.0)))
    mixed = jnp.sqrt(1.0 - loading)[:, None] * mixed + jnp.sqrt(loading)[:, None] * common[None, :]
    return jnp.clip(0.0625 * scale[:, None] * mixed, -1.0, 1.0).astype(jnp.bfloat16)


def shard_levels(key, dims, pieces, smallest, top_value):
    loudness, own = 1.0, jax.random.fold_in(key, 6)
    for dim, blocks in pieces:
        steps = jnp.exp(jax.random.uniform(jax.random.fold_in(own, dim), (blocks,), jnp.float32, smallest / len(pieces), top_value / len(pieces)))
        loudness = loudness * jnp.repeat(steps, dims[dim] // blocks).reshape([-1 if axis == dim else 1 for axis in range(len(dims))])
    return loudness


def setup_inputs(seed: int = 0) -> dict:
    streams_of = jax.random.split(jax.random.key(seed), 4)
    views = draw_views(jax.random.fold_in(streams_of[3], 71), 0)
    partner = draw_partner(jax.random.fold_in(streams_of[3], 71), 0)
    weight = jnp.clip(jnp.exp(math.log(4.0) - 2.7725887 * jax.random.uniform(streams_of[2], (NV,), jnp.float32) ** shard_levels(streams_of[2], (NV,), ((0, 16),), -0.2, 0.2)), 0.25, 4.0)
    return dict(views=views, partner=partner, weight=weight)


INV_TAU = 10.0
EPS = 1e-06

def reference(views, partner, weight):
    floats = views.astype(jnp.float32)
    length = jnp.sqrt(lax.optimization_barrier(jnp.sum(floats * floats, axis=1)) + EPS)
    unit = floats / length[:, None]
    normal = unit.astype(jnp.bfloat16)
    block = min(512, NV)
    count = NV // block
    col_ids = jnp.arange(NV, dtype=jnp.int32)

    def scores(index):
        start = (index * block).astype(jnp.int32)
        rows = lax.dynamic_slice_in_dim(normal, start, block, 0)
        s = jnp.dot(rows, normal.T, preferred_element_type=jnp.float32) * INV_TAU
        row_ids = start + jnp.arange(block, dtype=jnp.int32)
        mates = lax.dynamic_slice_in_dim(partner, start, block, 0)
        off = row_ids[:, None] != col_ids[None, :]
        match = mates[:, None] == col_ids[None, :]
        return (s, off, match, start)

    def first(index):
        s, off, match, start = scores(index)
        total = lax.optimization_barrier(jnp.sum(jnp.where(off, jnp.exp(s), jnp.float32(0.0)), axis=1))
        positive = lax.optimization_barrier(jnp.sum(jnp.where(match, s, jnp.float32(0.0)), axis=1))
        return (total, positive)
    total, positive = lax.map(first, jnp.arange(count, dtype=jnp.int32))
    lse = jnp.log(total.reshape(NV))
    loss = lse - positive.reshape(NV)

    def second(index):
        s, off, match, start = scores(index)
        lse_rows = lax.dynamic_slice_in_dim(lse, start, block, 0)
        w_rows = lax.dynamic_slice_in_dim(weight, start, block, 0)
        prow = jnp.exp(s - lse_rows[:, None])
        pcol = jnp.exp(s - lse[None, :])
        coef = jnp.where(off, w_rows[:, None] * prow + weight[None, :] * pcol, jnp.float32(0.0))
        coef = coef - jnp.where(match, w_rows[:, None] + weight[None, :], jnp.float32(0.0))
        coef = coef.astype(jnp.bfloat16)
        return jnp.dot(coef, normal, preferred_element_type=jnp.float32)
    g = lax.map(second, jnp.arange(count, dtype=jnp.int32)).reshape(NV, W) * INV_TAU
    grad = (g - unit * lax.optimization_barrier(jnp.sum(unit * g, axis=1, keepdims=True))) / length[:, None]
    return (loss, grad)
```

```python
import functools
import math

import jax
import jax.numpy as jnp
from jax import lax
from jax.experimental import pallas as pl
from jax.experimental.pallas import tpu as pltpu
from jax.sharding import PartitionSpec as P

INV_TAU = 10.0
EPS = 1e-06
SCALE = INV_TAU / math.log(2.0)
MESH = pl.DeviceIdType.MESH
EXTRA = 16


def fold(x):
    width = x.shape[1]
    if width <= 128:
        return x
    total = x[:, :128]
    for start in range(128, width, 128):
        total = total + x[:, start : start + 128]
    return total


def widen(x, width):
    if width <= 128:
        return x[:, :width]
    return jnp.concatenate([x] * (width // 128), axis=1)


def as_columns(row):
    return jnp.transpose(jnp.broadcast_to(row, (128, row.shape[1])))


def kernel(
    n,
    p,
    views_ref,
    partner_ref,
    weight_ref,
    loss_ref,
    grad_ref,
    rows_bf,
    cols,
    exps,
    scaled,
    acc_u,
    acc_p,
    acc_t,
    acc_w,
    mates,
    stats,
    all_a,
    parts,
    send_z,
    send_y,
    send_c,
    recv_b,
    send_s,
    recv_s,
    send_a,
    recv_a,
    send_g,
    recv_g,
):
    rows, width = views_ref.shape
    piece = rows // p
    chunk = min(128, rows)
    chunks = rows // chunk
    lanes = min(piece, 128)
    depth = n // 4
    me = lax.axis_index("dp")
    slot = lax.axis_index("mp")
    core = lax.rem(me, 2)
    y = lax.rem(lax.div(me, 2), 2)
    z = lax.div(me, 4)

    def place(zz, yy, cc):
        return (zz * 2 + yy) * 2 + cc

    barrier = pltpu.get_barrier_semaphore()

    def greet_dp(k, carry):
        pl.semaphore_signal(
            barrier, inc=1, device_id=(lax.rem(me + k, n), slot), device_id_type=MESH
        )
        return carry

    def greet_mp(k, carry):
        pl.semaphore_signal(
            barrier, inc=1, device_id=(me, lax.rem(slot + k, p)), device_id_type=MESH
        )
        return carry

    lax.fori_loop(1, n, greet_dp, 0)
    lax.fori_loop(1, p, greet_mp, 0)

    def lengths(i):
        at = pl.ds(i * chunk, chunk)
        floats = views_ref[at, :].astype(jnp.float32)
        length = jnp.sqrt(jnp.sum(floats * floats, axis=1, keepdims=True) + EPS)
        return floats, length

    for i in range(chunks):
        floats, length = lengths(i)
        rows_bf[i * chunk : (i + 1) * chunk, :] = (floats / length).astype(jnp.bfloat16)
    start = pl.multiple_of(slot * piece, piece)
    cols[me, 0:piece, :] = rows_bf[pl.ds(start, piece), :]
    weight_row = weight_ref[...]
    high = weight_row.astype(jnp.bfloat16).astype(jnp.float32)
    middle = (weight_row - high).astype(jnp.bfloat16).astype(jnp.float32)
    low = weight_row - high - middle
    terms = jnp.concatenate(
        [high, middle, low, jnp.zeros((EXTRA - 3, rows), jnp.float32)], axis=0
    ).astype(jnp.bfloat16)
    for j in range(p):

        @pl.when(slot == j)
        def _():
            cols[me, piece : piece + EXTRA, 0:piece] = terms[:, j * piece : (j + 1) * piece]

    pl.semaphore_wait(barrier, n + p - 2)

    def block_copy(b, send, device):
        return pltpu.make_async_remote_copy(
            src_ref=cols.at[b],
            dst_ref=cols.at[b],
            send_sem=send,
            recv_sem=recv_b.at[b],
            device_id=(device, slot),
            device_id_type=MESH,
        )

    def up(b):
        return block_copy(b, send_z.at[0, b], place(jnp.minimum(z + 1, depth - 1), y, core))

    def down(b):
        return block_copy(b, send_z.at[1, b], place(jnp.maximum(z - 1, 0), y, core))

    def across(b):
        return block_copy(b, send_y.at[b], place(z, 1 - y, core))

    def sibling(b):
        return block_copy(b, send_c.at[b], place(z, y, 1 - core))

    short = jnp.minimum(z, depth - 1 - z)
    long_below = z > depth - 1 - z

    def line(k):
        paired = k <= 2 * short
        step = jnp.where(paired, lax.div(k + 1, 2), k - short)
        below = jnp.where(paired, lax.rem(k, 2) == 1, long_below)
        return jnp.where(below, z - step, z + step)

    def goes_up(zz):
        return jnp.logical_and(zz <= z, z < depth - 1)

    def goes_down(zz):
        return jnp.logical_and(zz >= z, z > 0)

    def forward(zz, b):
        @pl.when(goes_up(zz))
        def _():
            up(b).start()

        @pl.when(goes_down(zz))
        def _():
            down(b).start()

        across(b).start()
        sibling(b).start()

    forward(z, me)

    acc_u[...] = jnp.zeros_like(acc_u)
    acc_p[...] = jnp.zeros_like(acc_p)
    acc_t[...] = jnp.zeros_like(acc_t)
    acc_w[...] = jnp.zeros_like(acc_w)
    mates[...] = as_columns(partner_ref[...].astype(jnp.float32))

    def compute(b, own):
        block = cols[b, 0:piece, :]
        carried = cols[b, piece : piece + EXTRA, :].astype(jnp.float32)[:, :piece]
        weights = carried[0:1] + carried[1:2] + carried[2:3]
        lane = lax.broadcasted_iota(jnp.int32, (1, piece), 1)
        ids = (lane + (b * rows + slot * piece)).astype(jnp.float32)
        for i in range(chunks):
            at = slice(i * chunk, (i + 1) * chunk)
            s = lax.dot_general(
                rows_bf[at, :],
                block,
                (((1,), (1,)), ((), ())),
                preferred_element_type=jnp.float32,
            )
            e = jnp.exp2(s * SCALE)
            if own:
                here = lax.broadcasted_iota(jnp.int32, (chunk, piece), 0) + i * chunk
                there = lax.broadcasted_iota(jnp.int32, (chunk, piece), 1) + slot * piece
                e = jnp.where(here == there, 0.0, e)
            acc_t[at, :] += fold(e)
            match = widen(mates[at, :], piece) == ids
            acc_w[at, :] += fold(jnp.where(match, weights, 0.0))
            hit = jnp.where(match, 1.0, 0.0).astype(jnp.bfloat16)
            rounded = e.astype(jnp.bfloat16)
            exps[b, at, :] = rounded
            acc_u[at, :] += jnp.dot(rounded, block, preferred_element_type=jnp.float32)
            acc_p[at, :] += jnp.dot(hit, block, preferred_element_type=jnp.float32)

    compute(me, True)

    def arrived(b):
        sibling(b).wait_recv()

    def late(k):
        zz = line(k)
        b = place(zz, 1 - y, core)
        arrived(b)
        sibling(b).start()

        def one(j, carry):
            yy = jnp.where(j == 1, y, 1 - y)
            cc = jnp.where(j == 0, core, 1 - core)
            b = place(zz, yy, cc)

            @pl.when(j > 0)
            def _():
                arrived(b)

            compute(b, False)
            return carry

        lax.fori_loop(0, 3, one, 0)

    def body(k, carry):
        @pl.when(k < depth)
        def _():
            zz = line(k)
            b = place(zz, y, core)
            arrived(b)
            forward(zz, b)
            compute(b, False)

        late(k - 1)
        return carry

    lax.fori_loop(1, depth + 1, body, 0)

    positive = []
    for i in range(chunks):
        at = slice(i * chunk, (i + 1) * chunk)
        positive.append(fold(rows_bf[at, :].astype(jnp.float32) * acc_p[at, :]))
    positive = jnp.concatenate(positive, axis=0)
    total_row = jnp.sum(jnp.transpose(acc_t[...]), axis=0, keepdims=True)
    positive_row = INV_TAU * jnp.sum(jnp.transpose(positive), axis=0, keepdims=True)
    stats[slot] = jnp.concatenate(
        [total_row, positive_row, jnp.zeros((6, rows), jnp.float32)], axis=0
    )

    def stats_copy(source, k):
        return pltpu.make_async_remote_copy(
            src_ref=stats.at[source],
            dst_ref=stats.at[source],
            send_sem=send_s.at[k],
            recv_sem=recv_s.at[source],
            device_id=(me, lax.rem(slot + k, p)),
            device_id_type=MESH,
        )

    for k in range(1, p):
        stats_copy(slot, k).start()
    for k in range(1, p):
        stats_copy(lax.rem(slot + k, p), k).wait_recv()
    both = stats[0]
    for j in range(1, p):
        both = both + stats[j]
    total_row = both[0:1]
    loss_ref[...] = jnp.log(total_row) - both[1:2]
    share_row = weight_row / total_row
    for j in range(p):

        @pl.when(slot == j)
        def _():
            all_a[me] = share_row[:, j * piece : (j + 1) * piece]

    def a_copy(source, k):
        return pltpu.make_async_remote_copy(
            src_ref=all_a.at[source],
            dst_ref=all_a.at[source],
            send_sem=send_a.at[k],
            recv_sem=recv_a.at[source],
            device_id=(lax.rem(me + k, n), slot),
            device_id_type=MESH,
        )

    def send_all(k, carry):
        a_copy(me, k).start()
        return carry

    lax.fori_loop(1, n, send_all, 0)

    share_col = as_columns(share_row)
    weight_col = as_columns(weight_row)
    for i in range(chunks):
        at = slice(i * chunk, (i + 1) * chunk)
        mate = jnp.sum(acc_w[at, :], axis=1, keepdims=True)
        acc_u[at, :] = (
            widen(share_col[at, :], width) * acc_u[at, :]
            - (widen(weight_col[at, :], width) + mate) * acc_p[at, :]
        )

    def scale(k, carry):
        d = lax.rem(me + k, n)

        @pl.when(k > 0)
        def _():
            a_copy(d, k).wait_recv()

        factor = widen(as_columns(all_a[d]), width)
        scaled[d] = (cols[d, 0:piece, :].astype(jnp.float32) * factor).astype(jnp.bfloat16)
        return carry

    lax.fori_loop(0, n, scale, 0)

    def g_copy(source, i, k):
        at = pl.ds(i * chunk, chunk)
        return pltpu.make_async_remote_copy(
            src_ref=parts.at[source, at],
            dst_ref=parts.at[source, at],
            send_sem=send_g.at[k, i],
            recv_sem=recv_g.at[source, i],
            device_id=(me, lax.rem(slot + k, p)),
            device_id_type=MESH,
        )

    for i in range(chunks):
        at = slice(i * chunk, (i + 1) * chunk)
        g = acc_u[at, :]
        for d in range(n):
            g = g + jnp.dot(exps[d, at, :], scaled[d], preferred_element_type=jnp.float32)
        g = g * INV_TAU
        floats, length = lengths(i)
        unit = floats / length
        along = jnp.sum(unit * g, axis=1, keepdims=True)
        parts[slot, at, :] = ((g - unit * along) / length).astype(jnp.bfloat16)
        for k in range(1, p):
            g_copy(slot, i, k).start()
    for i in range(chunks):
        at = slice(i * chunk, (i + 1) * chunk)
        for k in range(1, p):
            g_copy(lax.rem(slot + k, p), i, k).wait_recv()
        total = parts[0, at, :].astype(jnp.float32)
        for j in range(1, p):
            total = total + parts[j, at, :].astype(jnp.float32)
        grad_ref[at, :] = total

    def drain(k, carry):
        zz = line(k)
        b = place(zz, y, core)

        @pl.when(goes_up(zz))
        def _():
            up(b).wait_send()

        @pl.when(goes_down(zz))
        def _():
            down(b).wait_send()

        across(b).wait_send()
        sibling(b).wait_send()
        sibling(place(zz, 1 - y, core)).wait_send()
        return carry

    lax.fori_loop(0, depth, drain, 0)

    def drain_a(k, carry):
        a_copy(me, k).wait_send()
        return carry

    lax.fori_loop(1, n, drain_a, 0)
    for k in range(1, p):
        stats_copy(slot, k).wait_send()
        for i in range(chunks):
            g_copy(slot, i, k).wait_send()


def shards(n, p, views, partner, weight):
    rows, width = views.shape
    piece = rows // p
    lanes = min(piece, 128)
    chunks = rows // min(128, rows)
    dma = pltpu.SemaphoreType.DMA
    vmem = pl.BlockSpec(memory_space=pltpu.VMEM)
    loss, grad = pl.pallas_call(
        functools.partial(kernel, n, p),
        out_shape=(
            jax.ShapeDtypeStruct((1, rows), jnp.float32),
            jax.ShapeDtypeStruct((rows, width), jnp.float32),
        ),
        in_specs=[vmem] * 3,
        out_specs=(vmem, vmem),
        scratch_shapes=[
            pltpu.VMEM((rows, width), jnp.bfloat16),
            pltpu.VMEM((n, piece + EXTRA, width), jnp.bfloat16),
            pltpu.VMEM((n, rows, piece), jnp.bfloat16),
            pltpu.VMEM((n, piece, width), jnp.bfloat16),
            pltpu.VMEM((rows, width), jnp.float32),
            pltpu.VMEM((rows, width), jnp.float32),
            pltpu.VMEM((rows, lanes), jnp.float32),
            pltpu.VMEM((rows, lanes), jnp.float32),
            pltpu.VMEM((rows, 128), jnp.float32),
            pltpu.VMEM((p, 8, rows), jnp.float32),
            pltpu.VMEM((n, 1, piece), jnp.float32),
            pltpu.VMEM((p, rows, width), jnp.bfloat16),
            dma((2, n)),
            dma((n,)),
            dma((n,)),
            dma((n,)),
            dma((p,)),
            dma((p,)),
            dma((n,)),
            dma((n,)),
            dma((p, chunks)),
            dma((p, chunks)),
        ],
        compiler_params=pltpu.CompilerParams(
            collective_id=0, has_side_effects=True, vmem_limit_bytes=40 * 1024 * 1024
        ),
    )(views, partner.reshape(1, rows), weight.reshape(1, rows))
    return loss.reshape(rows), grad


def solution(mesh):
    n, p = mesh.shape["dp"], mesh.shape["mp"]
    return jax.shard_map(
        functools.partial(shards, n, p),
        mesh=mesh,
        in_specs=(P("dp", None), P("dp"), P("dp")),
        out_specs=(P("dp"), P("dp", None)),
        check_vma=False,
    )
```

```python
import functools
import math

import jax
import jax.numpy as jnp
from jax import lax
from jax.experimental import pallas as pl
from jax.experimental.pallas import tpu as pltpu
from jax.sharding import PartitionSpec as P

INV_TAU = 10.0
EPS = 1e-06
SCALE = INV_TAU / math.log(2.0)
MESH = pl.DeviceIdType.MESH
SUBS = 4
EXTRA = 16


def fold(x):
    width = x.shape[1]
    if width <= 128:
        return x
    total = x[:, :128]
    for start in range(128, width, 128):
        total = total + x[:, start : start + 128]
    return total


def widen(x, width):
    if width <= 128:
        return x[:, :width]
    return jnp.concatenate([x] * (width // 128), axis=1)


def as_columns(row):
    return jnp.transpose(jnp.broadcast_to(row, (128, row.shape[1])))


def kernel(
    n,
    p,
    views_ref,
    partner_ref,
    weight_ref,
    loss_ref,
    grad_ref,
    rows_bf,
    cols,
    exps,
    scaled,
    acc_u,
    acc_p,
    acc_t,
    acc_w,
    mates,
    stats,
    all_a,
    parts,
    send_z,
    send_y,
    send_c,
    recv_b,
    send_s,
    recv_s,
    send_a,
    recv_a,
    send_g,
    recv_g,
):
    rows, width = views_ref.shape
    piece = rows // p
    chunk = min(128, rows)
    chunks = rows // chunk
    lanes = min(piece, 128)
    depth = n // 4
    me = lax.axis_index("dp")
    slot = lax.axis_index("mp")
    core = lax.rem(me, 2)
    y = lax.rem(lax.div(me, 2), 2)
    z = lax.div(me, 4)

    def place(zz, yy, cc):
        return (zz * 2 + yy) * 2 + cc

    barrier = pltpu.get_barrier_semaphore()

    def greet(device):
        pl.semaphore_signal(barrier, inc=1, device_id=(device, slot), device_id_type=MESH)

    greet(place(z, y, 1 - core))
    greet(place(z, 1 - y, core))

    @pl.when(z < depth - 1)
    def _():
        greet(place(z + 1, y, core))

    @pl.when(z > 0)
    def _():
        greet(place(z - 1, y, core))

    def greet_mp(k, carry):
        pl.semaphore_signal(
            barrier, inc=1, device_id=(me, lax.rem(slot + k, p)), device_id_type=MESH
        )
        return carry

    lax.fori_loop(1, p, greet_mp, 0)

    def lengths(start, count):
        floats = views_ref[pl.ds(start, count), :].astype(jnp.float32)
        length = jnp.sqrt(jnp.sum(floats * floats, axis=1, keepdims=True) + EPS)
        return floats, length

    part = min(chunk, piece)
    for i in range(piece // part):
        start = pl.multiple_of(slot * piece + i * part, part)
        floats, length = lengths(start, part)
        at = slice(EXTRA + i * part, EXTRA + (i + 1) * part)
        cols[me, at, :] = (floats / length).astype(jnp.bfloat16)
    weight_row = weight_ref[...]
    high = weight_row.astype(jnp.bfloat16).astype(jnp.float32)
    middle = (weight_row - high).astype(jnp.bfloat16).astype(jnp.float32)
    low = weight_row - high - middle
    terms = jnp.concatenate(
        [high, middle, low, jnp.zeros((EXTRA - 3, rows), jnp.float32)], axis=0
    ).astype(jnp.bfloat16)
    for j in range(p):

        @pl.when(slot == j)
        def _():
            cols[me, 0:EXTRA, 0:piece] = terms[:, j * piece : (j + 1) * piece]

    ends = jnp.where(z == 0, 1, 0) + jnp.where(z == depth - 1, 1, 0)
    pl.semaphore_wait(barrier, 4 + p - 1 - ends)

    sub = piece // SUBS

    def block_copy(b, j, send, device):
        at = pl.ds(0, EXTRA + sub) if j == 0 else pl.ds(EXTRA + j * sub, sub)
        return pltpu.make_async_remote_copy(
            src_ref=cols.at[b, at],
            dst_ref=cols.at[b, at],
            send_sem=send,
            recv_sem=recv_b.at[b, j],
            device_id=(device, slot),
            device_id_type=MESH,
        )

    def up(b, j):
        return block_copy(b, j, send_z.at[0, b, j], place(jnp.minimum(z + 1, depth - 1), y, core))

    def down(b, j):
        return block_copy(b, j, send_z.at[1, b, j], place(jnp.maximum(z - 1, 0), y, core))

    def across(b, j):
        return block_copy(b, j, send_y.at[b, j], place(z, 1 - y, core))

    def sibling(b, j):
        return block_copy(b, j, send_c.at[b, j], place(z, y, 1 - core))

    short = jnp.minimum(z, depth - 1 - z)
    long_below = z > depth - 1 - z

    def line(k):
        paired = k <= 2 * short
        step = jnp.where(paired, lax.div(k + 1, 2), k - short)
        below = jnp.where(paired, lax.rem(k, 2) == 1, long_below)
        return jnp.where(below, z - step, z + step)

    def goes_up(zz):
        return jnp.logical_and(zz <= z, z < depth - 1)

    def goes_down(zz):
        return jnp.logical_and(zz >= z, z > 0)

    def forward(zz, b, j):
        @pl.when(goes_up(zz))
        def _():
            up(b, j).start()

        @pl.when(goes_down(zz))
        def _():
            down(b, j).start()

        across(b, j).start()
        sibling(b, j).start()

    for j in range(SUBS):
        forward(z, me, j)

    for i in range(chunks):
        floats, length = lengths(i * chunk, chunk)
        rows_bf[i * chunk : (i + 1) * chunk, :] = (floats / length).astype(jnp.bfloat16)
    acc_u[...] = jnp.zeros_like(acc_u)
    acc_p[...] = jnp.zeros_like(acc_p)
    acc_t[...] = jnp.zeros_like(acc_t)
    acc_w[...] = jnp.zeros_like(acc_w)
    mates[...] = as_columns(partner_ref[...].astype(jnp.float32))

    def compute(b, own):
        block = cols[b, EXTRA : EXTRA + piece, :]
        carried = cols[b, 0:EXTRA, :].astype(jnp.float32)[:, :piece]
        weights = carried[0:1] + carried[1:2] + carried[2:3]
        lane = lax.broadcasted_iota(jnp.int32, (1, piece), 1)
        ids = (lane + (b * rows + slot * piece)).astype(jnp.float32)
        for i in range(chunks):
            at = slice(i * chunk, (i + 1) * chunk)
            s = lax.dot_general(
                rows_bf[at, :],
                block,
                (((1,), (1,)), ((), ())),
                preferred_element_type=jnp.float32,
            )
            e = jnp.exp2(s * SCALE)
            if own:
                here = lax.broadcasted_iota(jnp.int32, (chunk, piece), 0) + i * chunk
                there = lax.broadcasted_iota(jnp.int32, (chunk, piece), 1) + slot * piece
                e = jnp.where(here == there, 0.0, e)
            acc_t[at, :] += fold(e)
            match = widen(mates[at, :], piece) == ids
            acc_w[at, :] += fold(jnp.where(match, weights, 0.0))
            hit = jnp.where(match, 1.0, 0.0).astype(jnp.bfloat16)
            rounded = e.astype(jnp.bfloat16)
            exps[b, at, :] = rounded
            acc_u[at, :] += jnp.dot(rounded, block, preferred_element_type=jnp.float32)
            acc_p[at, :] += jnp.dot(hit, block, preferred_element_type=jnp.float32)

    def arrived(b, j):
        sibling(b, j).wait_recv()

    def body(t, carry):
        ahead = line(t + 1)
        now = line(t)
        before = line(t - 1)
        for j in range(SUBS):

            @pl.when(t < depth - 1)
            def _():
                b = place(ahead, y, core)
                arrived(b, j)
                forward(ahead, b, j)

            @pl.when(t < depth)
            def _():
                b = place(now, 1 - y, core)
                arrived(b, j)
                sibling(b, j).start()

            if j == 0:

                @pl.when(t == 0)
                def _():
                    compute(me, True)

                @pl.when(jnp.logical_and(t > 0, t < depth))
                def _():
                    compute(place(now, y, core), False)

            if j == 1:

                @pl.when(t > 0)
                def _():
                    compute(place(before, 1 - y, core), False)

            if j == 2:

                @pl.when(t < depth)
                def _():
                    b = place(now, y, 1 - core)
                    for q in range(SUBS):
                        arrived(b, q)
                    compute(b, False)

            if j == 3:

                @pl.when(t > 0)
                def _():
                    b = place(before, 1 - y, 1 - core)
                    for q in range(SUBS):
                        arrived(b, q)
                    compute(b, False)

        return carry

    lax.fori_loop(0, depth + 1, body, 0)

    positive = []
    for i in range(chunks):
        at = slice(i * chunk, (i + 1) * chunk)
        positive.append(fold(rows_bf[at, :].astype(jnp.float32) * acc_p[at, :]))
    positive = jnp.concatenate(positive, axis=0)
    total_row = jnp.sum(jnp.transpose(acc_t[...]), axis=0, keepdims=True)
    positive_row = INV_TAU * jnp.sum(jnp.transpose(positive), axis=0, keepdims=True)
    stats[slot] = jnp.concatenate(
        [total_row, positive_row], axis=0
    )

    def stats_copy(source, k):
        return pltpu.make_async_remote_copy(
            src_ref=stats.at[source],
            dst_ref=stats.at[source],
            send_sem=send_s.at[k],
            recv_sem=recv_s.at[source],
            device_id=(me, lax.rem(slot + k, p)),
            device_id_type=MESH,
        )

    for k in range(1, p):
        stats_copy(slot, k).start()
    for k in range(1, p):
        stats_copy(lax.rem(slot + k, p), k).wait_recv()
    both = stats[0]
    for j in range(1, p):
        both = both + stats[j]
    total_row = both[0:1]
    loss_ref[...] = jnp.log(total_row) - both[1:2]
    share_row = weight_row / total_row
    for j in range(p):

        @pl.when(slot == j)
        def _():
            all_a[me] = share_row[:, j * piece : (j + 1) * piece]

    def a_copy(source, k):
        return pltpu.make_async_remote_copy(
            src_ref=all_a.at[source],
            dst_ref=all_a.at[source],
            send_sem=send_a.at[k],
            recv_sem=recv_a.at[source],
            device_id=(lax.rem(me + k, n), slot),
            device_id_type=MESH,
        )

    def send_all(k, carry):
        a_copy(me, k).start()
        return carry

    lax.fori_loop(1, n, send_all, 0)

    share_col = as_columns(share_row)
    weight_col = as_columns(weight_row)
    for i in range(chunks):
        at = slice(i * chunk, (i + 1) * chunk)
        mate = jnp.sum(acc_w[at, :], axis=1, keepdims=True)
        acc_u[at, :] = (
            widen(share_col[at, :], width) * acc_u[at, :]
            - (widen(weight_col[at, :], width) + mate) * acc_p[at, :]
        )

    def scale(k, carry):
        d = lax.rem(me + k, n)

        @pl.when(k > 0)
        def _():
            a_copy(d, k).wait_recv()

        factor = widen(as_columns(all_a[d]), width)
        scaled[d] = (cols[d, EXTRA : EXTRA + piece, :].astype(jnp.float32) * factor).astype(jnp.bfloat16)
        return carry

    lax.fori_loop(0, n, scale, 0)

    def g_copy(source, i, k):
        at = pl.ds(i * chunk, chunk)
        return pltpu.make_async_remote_copy(
            src_ref=parts.at[source, at],
            dst_ref=parts.at[source, at],
            send_sem=send_g.at[k, i],
            recv_sem=recv_g.at[source, i],
            device_id=(me, lax.rem(slot + k, p)),
            device_id_type=MESH,
        )

    for i in range(chunks):
        at = slice(i * chunk, (i + 1) * chunk)
        g = acc_u[at, :]
        for d in range(n):
            g = g + jnp.dot(exps[d, at, :], scaled[d], preferred_element_type=jnp.float32)
        g = g * INV_TAU
        floats, length = lengths(i * chunk, chunk)
        unit = floats / length
        along = jnp.sum(unit * g, axis=1, keepdims=True)
        parts[slot, at, :] = ((g - unit * along) / length).astype(jnp.bfloat16)
        for k in range(1, p):
            g_copy(slot, i, k).start()
    def drain(k, carry):
        zz = line(k)
        b = place(zz, y, core)
        other = place(zz, 1 - y, core)
        for j in range(SUBS):

            @pl.when(goes_up(zz))
            def _():
                up(b, j).wait_send()

            @pl.when(goes_down(zz))
            def _():
                down(b, j).wait_send()

            across(b, j).wait_send()
            sibling(b, j).wait_send()
            sibling(other, j).wait_send()
        return carry

    lax.fori_loop(0, depth, drain, 0)

    def drain_a(k, carry):
        a_copy(me, k).wait_send()
        return carry

    lax.fori_loop(1, n, drain_a, 0)
    for k in range(1, p):
        stats_copy(slot, k).wait_send()

    for i in range(chunks):
        at = slice(i * chunk, (i + 1) * chunk)
        for k in range(1, p):
            g_copy(lax.rem(slot + k, p), i, k).wait_recv()
        total = parts[0, at, :].astype(jnp.float32)
        for j in range(1, p):
            total = total + parts[j, at, :].astype(jnp.float32)
        grad_ref[at, :] = total
    for k in range(1, p):
        for i in range(chunks):
            g_copy(slot, i, k).wait_send()


def shards(n, p, views, partner, weight):
    rows, width = views.shape
    piece = rows // p
    lanes = min(piece, 128)
    chunks = rows // min(128, rows)
    dma = pltpu.SemaphoreType.DMA
    vmem = pl.BlockSpec(memory_space=pltpu.VMEM)
    loss, grad = pl.pallas_call(
        functools.partial(kernel, n, p),
        out_shape=(
            jax.ShapeDtypeStruct((1, rows), jnp.float32),
            jax.ShapeDtypeStruct((rows, width), jnp.float32),
        ),
        in_specs=[vmem] * 3,
        out_specs=(vmem, vmem),
        scratch_shapes=[
            pltpu.VMEM((rows, width), jnp.bfloat16),
            pltpu.VMEM((n, piece + EXTRA, width), jnp.bfloat16),
            pltpu.VMEM((n, rows, piece), jnp.bfloat16),
            pltpu.VMEM((n, piece, width), jnp.bfloat16),
            pltpu.VMEM((rows, width), jnp.float32),
            pltpu.VMEM((rows, width), jnp.float32),
            pltpu.VMEM((rows, lanes), jnp.float32),
            pltpu.VMEM((rows, lanes), jnp.float32),
            pltpu.VMEM((rows, 128), jnp.float32),
            pltpu.VMEM((p, 2, rows), jnp.float32),
            pltpu.VMEM((n, 1, piece), jnp.float32),
            pltpu.VMEM((p, rows, width), jnp.bfloat16),
            dma((2, n, SUBS)),
            dma((n, SUBS)),
            dma((n, SUBS)),
            dma((n, SUBS)),
            dma((p,)),
            dma((p,)),
            dma((n,)),
            dma((n,)),
            dma((p, chunks)),
            dma((p, chunks)),
        ],
        compiler_params=pltpu.CompilerParams(
            collective_id=0, has_side_effects=True, vmem_limit_bytes=48 * 1024 * 1024
        ),
    )(views, partner.reshape(1, rows), weight.reshape(1, rows))
    return loss.reshape(rows), grad


def solution(mesh):
    n, p = mesh.shape["dp"], mesh.shape["mp"]
    return jax.shard_map(
        functools.partial(shards, n, p),
        mesh=mesh,
        in_specs=(P("dp", None), P("dp"), P("dp")),
        out_specs=(P("dp"), P("dp", None)),
        check_vma=False,
    )
```

```python
import functools
import math

import jax
import jax.numpy as jnp
from jax import lax
from jax.experimental import pallas as pl
from jax.experimental.pallas import tpu as pltpu
from jax.sharding import PartitionSpec as P

INV_TAU = 10.0
EPS = 1e-06
SCALE = INV_TAU / math.log(2.0)
MESH = pl.DeviceIdType.MESH
SUBS = 4
EXTRA = 16


def fold(x):
    width = x.shape[1]
    if width <= 128:
        return x
    total = x[:, :128]
    for start in range(128, width, 128):
        total = total + x[:, start : start + 128]
    return total


def widen(x, width):
    if width <= 128:
        return x[:, :width]
    return jnp.concatenate([x] * (width // 128), axis=1)


def as_columns(row):
    return jnp.transpose(jnp.broadcast_to(row, (128, row.shape[1])))


def kernel(
    n,
    p,
    views_ref,
    partner_ref,
    weight_ref,
    loss_ref,
    grad_ref,
    rows_bf,
    cols,
    exps,
    scaled,
    acc_u,
    acc_p,
    acc_t,
    acc_w,
    mates,
    stats,
    all_a,
    parts,
    send_z,
    send_y,
    send_c,
    recv_b,
    send_s,
    recv_s,
    send_a,
    recv_a,
    send_g,
    recv_g,
):
    rows, width = views_ref.shape
    piece = rows // p
    chunk = min(128, rows)
    chunks = rows // chunk
    lanes = min(piece, 128)
    depth = n // 4
    me = lax.axis_index("dp")
    slot = lax.axis_index("mp")
    core = lax.rem(me, 2)
    y = lax.rem(lax.div(me, 2), 2)
    z = lax.div(me, 4)

    def place(zz, yy, cc):
        return (zz * 2 + yy) * 2 + cc

    barrier = pltpu.get_barrier_semaphore()

    def greet(device):
        pl.semaphore_signal(barrier, inc=1, device_id=(device, slot), device_id_type=MESH)

    greet(place(z, y, 1 - core))
    greet(place(z, 1 - y, core))

    @pl.when(z < depth - 1)
    def _():
        greet(place(z + 1, y, core))

    @pl.when(z > 0)
    def _():
        greet(place(z - 1, y, core))

    def greet_mp(k, carry):
        pl.semaphore_signal(
            barrier, inc=1, device_id=(me, lax.rem(slot + k, p)), device_id_type=MESH
        )
        return carry

    lax.fori_loop(1, p, greet_mp, 0)

    def lengths(start, count):
        floats = views_ref[pl.ds(start, count), :].astype(jnp.float32)
        length = jnp.sqrt(jnp.sum(floats * floats, axis=1, keepdims=True) + EPS)
        return floats, length

    part = min(chunk, piece)
    for i in range(piece // part):
        start = pl.multiple_of(slot * piece + i * part, part)
        floats, length = lengths(start, part)
        at = slice(EXTRA + i * part, EXTRA + (i + 1) * part)
        cols[me, at, :] = (floats / length).astype(jnp.bfloat16)
    weight_row = weight_ref[...]
    high = weight_row.astype(jnp.bfloat16).astype(jnp.float32)
    middle = (weight_row - high).astype(jnp.bfloat16).astype(jnp.float32)
    low = weight_row - high - middle
    terms = jnp.concatenate(
        [high, middle, low, jnp.zeros((EXTRA - 3, rows), jnp.float32)], axis=0
    ).astype(jnp.bfloat16)
    for j in range(p):

        @pl.when(slot == j)
        def _():
            cols[me, 0:EXTRA, 0:piece] = terms[:, j * piece : (j + 1) * piece]

    ends = jnp.where(z == 0, 1, 0) + jnp.where(z == depth - 1, 1, 0)
    pl.semaphore_wait(barrier, 4 + p - 1 - ends)

    sub = piece // SUBS

    def block_copy(b, j, send, device):
        at = pl.ds(0, EXTRA + sub) if j == 0 else pl.ds(EXTRA + j * sub, sub)
        return pltpu.make_async_remote_copy(
            src_ref=cols.at[b, at],
            dst_ref=cols.at[b, at],
            send_sem=send,
            recv_sem=recv_b.at[b, j],
            device_id=(device, slot),
            device_id_type=MESH,
        )

    def up(b, j):
        return block_copy(b, j, send_z.at[0, b, j], place(jnp.minimum(z + 1, depth - 1), y, core))

    def down(b, j):
        return block_copy(b, j, send_z.at[1, b, j], place(jnp.maximum(z - 1, 0), y, core))

    def across(b, j):
        return block_copy(b, j, send_y.at[b, j], place(z, 1 - y, core))

    def sibling(b, j):
        return block_copy(b, j, send_c.at[b, j], place(z, y, 1 - core))

    short = jnp.minimum(z, depth - 1 - z)
    long_below = z > depth - 1 - z

    def line(k):
        paired = k <= 2 * short
        step = jnp.where(paired, lax.div(k + 1, 2), k - short)
        below = jnp.where(paired, lax.rem(k, 2) == 1, long_below)
        return jnp.where(below, z - step, z + step)

    def goes_up(zz):
        return jnp.logical_and(zz <= z, z < depth - 1)

    def goes_down(zz):
        return jnp.logical_and(zz >= z, z > 0)

    def forward(zz, b, j):
        across(b, j).start()

        @pl.when(goes_up(zz))
        def _():
            up(b, j).start()

        @pl.when(goes_down(zz))
        def _():
            down(b, j).start()

        sibling(b, j).start()

    for j in range(SUBS):
        forward(z, me, j)

    for i in range(chunks):
        floats, length = lengths(i * chunk, chunk)
        rows_bf[i * chunk : (i + 1) * chunk, :] = (floats / length).astype(jnp.bfloat16)
    acc_u[...] = jnp.zeros_like(acc_u)
    acc_p[...] = jnp.zeros_like(acc_p)
    acc_t[...] = jnp.zeros_like(acc_t)
    acc_w[...] = jnp.zeros_like(acc_w)
    mates[...] = as_columns(partner_ref[...].astype(jnp.float32))

    def compute(b, own):
        block = cols[b, EXTRA : EXTRA + piece, :]
        carried = cols[b, 0:EXTRA, :].astype(jnp.float32)[:, :piece]
        weights = carried[0:1] + carried[1:2] + carried[2:3]
        lane = lax.broadcasted_iota(jnp.int32, (1, piece), 1)
        ids = (lane + (b * rows + slot * piece)).astype(jnp.float32)
        for i in range(chunks):
            at = slice(i * chunk, (i + 1) * chunk)
            s = lax.dot_general(
                rows_bf[at, :],
                block,
                (((1,), (1,)), ((), ())),
                preferred_element_type=jnp.float32,
            )
            e = jnp.exp2(s * SCALE)
            if own:
                here = lax.broadcasted_iota(jnp.int32, (chunk, piece), 0) + i * chunk
                there = lax.broadcasted_iota(jnp.int32, (chunk, piece), 1) + slot * piece
                e = jnp.where(here == there, 0.0, e)
            acc_t[at, :] += fold(e)
            match = widen(mates[at, :], piece) == ids
            acc_w[at, :] += fold(jnp.where(match, weights, 0.0))
            hit = jnp.where(match, 1.0, 0.0).astype(jnp.bfloat16)
            rounded = e.astype(jnp.bfloat16)
            exps[b, at, :] = rounded
            acc_u[at, :] += jnp.dot(rounded, block, preferred_element_type=jnp.float32)
            acc_p[at, :] += jnp.dot(hit, block, preferred_element_type=jnp.float32)

    def arrived(b, j):
        sibling(b, j).wait_recv()

    def body(t, carry):
        ahead = line(t + 1)
        now = line(t)
        before = line(t - 1)
        for j in range(SUBS):

            @pl.when(t < depth - 1)
            def _():
                b = place(ahead, y, core)
                arrived(b, j)
                forward(ahead, b, j)

            @pl.when(t < depth)
            def _():
                b = place(now, 1 - y, core)
                arrived(b, j)
                sibling(b, j).start()

            if j == 0:

                @pl.when(t == 0)
                def _():
                    compute(me, True)

                @pl.when(jnp.logical_and(t > 0, t < depth))
                def _():
                    compute(place(now, y, core), False)

            if j == 1:

                @pl.when(t > 0)
                def _():
                    compute(place(before, 1 - y, core), False)

            if j == 2:

                @pl.when(t < depth)
                def _():
                    b = place(now, y, 1 - core)
                    for q in range(SUBS):
                        arrived(b, q)
                    compute(b, False)

            if j == 3:

                @pl.when(t > 0)
                def _():
                    b = place(before, 1 - y, 1 - core)
                    for q in range(SUBS):
                        arrived(b, q)
                    compute(b, False)

        return carry

    lax.fori_loop(0, depth + 1, body, 0)

    def stats_copy(what, source, k):
        return pltpu.make_async_remote_copy(
            src_ref=stats.at[what, source],
            dst_ref=stats.at[what, source],
            send_sem=send_s.at[what, k],
            recv_sem=recv_s.at[what, source],
            device_id=(me, lax.rem(slot + k, p)),
            device_id_type=MESH,
        )

    def stats_sum(what):
        for k in range(1, p):
            stats_copy(what, lax.rem(slot + k, p), k).wait_recv()
        result = stats[what, 0]
        for j in range(1, p):
            result = result + stats[what, j]
        return result

    stats[0, slot] = jnp.sum(jnp.transpose(acc_t[...]), axis=0, keepdims=True)
    for k in range(1, p):
        stats_copy(0, slot, k).start()
    positive = []
    for i in range(chunks):
        at = slice(i * chunk, (i + 1) * chunk)
        positive.append(fold(rows_bf[at, :].astype(jnp.float32) * acc_p[at, :]))
    positive = jnp.concatenate(positive, axis=0)
    stats[1, slot] = INV_TAU * jnp.sum(jnp.transpose(positive), axis=0, keepdims=True)
    for k in range(1, p):
        stats_copy(1, slot, k).start()
    weight_col = as_columns(weight_row)
    for i in range(chunks):
        at = slice(i * chunk, (i + 1) * chunk)
        mate = jnp.sum(acc_w[at, :], axis=1, keepdims=True)
        acc_p[at, :] = (widen(weight_col[at, :], width) + mate) * acc_p[at, :]
    total_row = stats_sum(0)
    share_row = weight_row / total_row
    for j in range(p):

        @pl.when(slot == j)
        def _():
            all_a[me] = share_row[:, j * piece : (j + 1) * piece]

    def a_copy(source, k):
        return pltpu.make_async_remote_copy(
            src_ref=all_a.at[source],
            dst_ref=all_a.at[source],
            send_sem=send_a.at[k],
            recv_sem=recv_a.at[source],
            device_id=(lax.rem(me + k, n), slot),
            device_id_type=MESH,
        )

    def send_all(k, carry):
        a_copy(me, k).start()
        return carry

    lax.fori_loop(1, n, send_all, 0)

    share_col = as_columns(share_row)
    loss_ref[...] = jnp.log(total_row) - stats_sum(1)
    for i in range(chunks):
        at = slice(i * chunk, (i + 1) * chunk)
        acc_u[at, :] = (
            widen(share_col[at, :], width) * acc_u[at, :]
            - acc_p[at, :]
        )

    def scale(k, carry):
        d = lax.rem(me + k, n)

        @pl.when(k > 0)
        def _():
            a_copy(d, k).wait_recv()

        factor = widen(as_columns(all_a[d]), width)
        scaled[d] = (cols[d, EXTRA : EXTRA + piece, :].astype(jnp.float32) * factor).astype(jnp.bfloat16)
        return carry

    lax.fori_loop(0, n, scale, 0)

    def g_copy(source, i, k):
        at = pl.ds(i * chunk, chunk)
        return pltpu.make_async_remote_copy(
            src_ref=parts.at[source, at],
            dst_ref=parts.at[source, at],
            send_sem=send_g.at[k, i],
            recv_sem=recv_g.at[source, i],
            device_id=(me, lax.rem(slot + k, p)),
            device_id_type=MESH,
        )

    for i in range(chunks):
        at = slice(i * chunk, (i + 1) * chunk)
        g = acc_u[at, :]
        for d in range(n):
            g = g + jnp.dot(exps[d, at, :], scaled[d], preferred_element_type=jnp.float32)
        g = g * INV_TAU
        floats, length = lengths(i * chunk, chunk)
        unit = floats / length
        along = jnp.sum(unit * g, axis=1, keepdims=True)
        parts[slot, at, :] = ((g - unit * along) / length).astype(jnp.bfloat16)
        for k in range(1, p):
            g_copy(slot, i, k).start()
    def drain(k, carry):
        zz = line(k)
        b = place(zz, y, core)
        other = place(zz, 1 - y, core)
        for j in range(SUBS):

            @pl.when(goes_up(zz))
            def _():
                up(b, j).wait_send()

            @pl.when(goes_down(zz))
            def _():
                down(b, j).wait_send()

            across(b, j).wait_send()
            sibling(b, j).wait_send()
            sibling(other, j).wait_send()
        return carry

    lax.fori_loop(0, depth, drain, 0)

    def drain_a(k, carry):
        a_copy(me, k).wait_send()
        return carry

    lax.fori_loop(1, n, drain_a, 0)
    for k in range(1, p):
        stats_copy(0, slot, k).wait_send()
        stats_copy(1, slot, k).wait_send()

    for i in range(chunks):
        at = slice(i * chunk, (i + 1) * chunk)
        for k in range(1, p):
            g_copy(lax.rem(slot + k, p), i, k).wait_recv()
        total = parts[0, at, :].astype(jnp.float32)
        for j in range(1, p):
            total = total + parts[j, at, :].astype(jnp.float32)
        grad_ref[at, :] = total
    for k in range(1, p):
        for i in range(chunks):
            g_copy(slot, i, k).wait_send()


def shards(n, p, views, partner, weight):
    rows, width = views.shape
    piece = rows // p
    lanes = min(piece, 128)
    chunks = rows // min(128, rows)
    dma = pltpu.SemaphoreType.DMA
    vmem = pl.BlockSpec(memory_space=pltpu.VMEM)
    loss, grad = pl.pallas_call(
        functools.partial(kernel, n, p),
        out_shape=(
            jax.ShapeDtypeStruct((1, rows), jnp.float32),
            jax.ShapeDtypeStruct((rows, width), jnp.float32),
        ),
        in_specs=[vmem] * 3,
        out_specs=(vmem, vmem),
        scratch_shapes=[
            pltpu.VMEM((rows, width), jnp.bfloat16),
            pltpu.VMEM((n, piece + EXTRA, width), jnp.bfloat16),
            pltpu.VMEM((n, rows, piece), jnp.bfloat16),
            pltpu.VMEM((n, piece, width), jnp.bfloat16),
            pltpu.VMEM((rows, width), jnp.float32),
            pltpu.VMEM((rows, width), jnp.float32),
            pltpu.VMEM((rows, lanes), jnp.float32),
            pltpu.VMEM((rows, lanes), jnp.float32),
            pltpu.VMEM((rows, 128), jnp.float32),
            pltpu.VMEM((2, p, 1, rows), jnp.float32),
            pltpu.VMEM((n, 1, piece), jnp.float32),
            pltpu.VMEM((p, rows, width), jnp.bfloat16),
            dma((2, n, SUBS)),
            dma((n, SUBS)),
            dma((n, SUBS)),
            dma((n, SUBS)),
            dma((2, p)),
            dma((2, p)),
            dma((n,)),
            dma((n,)),
            dma((p, chunks)),
            dma((p, chunks)),
        ],
        compiler_params=pltpu.CompilerParams(
            collective_id=0, has_side_effects=True, vmem_limit_bytes=48 * 1024 * 1024
        ),
    )(views, partner.reshape(1, rows), weight.reshape(1, rows))
    return loss.reshape(rows), grad


def solution(mesh):
    n, p = mesh.shape["dp"], mesh.shape["mp"]
    return jax.shard_map(
        functools.partial(shards, n, p),
        mesh=mesh,
        in_specs=(P("dp", None), P("dp"), P("dp")),
        out_specs=(P("dp"), P("dp", None)),
        check_vma=False,
    )
```
